32 devices in a mesh: ta: 4 (over x, core), ha: 4 (over z), ga: 2 (over y).
Axes of the slice: x: 2, y: 2, z: 4, core: 2. Of those that a mesh axis runs over, the one named last changes fastest.
Arguments:
- query_in: bfloat16 [12, 4, 8, 8, 512], P('ta', 'ha', None, None, 'ga'), may hold values from -6 to 6
- key_in: bfloat16 [12, 4, 8, 8, 512], P('ta', 'ha', None, None, 'ga'), may hold values from -6.0625 to 6.0625
- value_in: bfloat16 [12, 4, 8, 8, 512], P('ta', 'ha', None, None, 'ga'), may hold values from -6 to 6
- saved_out: bfloat16 [12, 4, 8, 8, 512], P('ta', 'ha', None, None, 'ga'), may hold values from -6 to 6
- out_grad: bfloat16 [12, 4, 8, 8, 512], P('ta', 'ha', None, None, 'ga'), may hold values from -6 to 6
- window_mask: int32 [2, 1, 4, 27], replicated, may hold values from 0 to 1, as said below
Outputs:
- query_grad: bfloat16 [12, 4, 8, 8, 512], P('ta', 'ha', None, None, 'ga')
- key_grad: bfloat16 [12, 4, 8, 8, 512], P('ta', 'ha', None, None, 'ga')
- value_grad: bfloat16 [12, 4, 8, 8, 512], P('ta', 'ha', None, None, 'ga')
The draws below stay inside these ranges and needn't reach their ends.
Inputs may be any that keep to these rules, and one draw needn't show every extreme that they name: `window_mask`: entry 13 (the tile itself) is 1 for every tile.
All inputs are finite; a program needn't handle non-finite values.
Results may differ from the reference program's by a relative error of at most 0.0058.
Values may be sent and summed in bfloat16 or wider, within the bound.
A program may use at most 128 MiB of HBM per device.

```python
import jax
import jax.numpy as jnp
from jax import lax

HEAD_DIM = 128
HEADS = 4
TILE_T = 6
TILE_H = 8
TILE_W = 8
FRAMES_DEV = 3
FRAMES = 12
W_TILES = 4
H_TILES = 1
PLANE_TILES = 4
T_TILES = 2
HD = 512
N_TA = 4
N_HA = 4


def draw_query_in(key, part):
    key = jax.random.fold_in(key, 1)
    full_shape = (FRAMES, PLANE_TILES, TILE_H, TILE_W, HEADS * HEAD_DIM)
    values = jnp.clip(jax.random.normal(key, full_shape, jnp.float32), -6.0, 6.0)
    return values.astype(jnp.bfloat16)


def draw_key_in(key, part):
    key = jax.random.fold_in(key, 2)
    full_shape = (FRAMES, PLANE_TILES, TILE_H, TILE_W, HEADS * HEAD_DIM)
    values = jnp.clip(jax.random.normal(key, full_shape, jnp.float32), -6.0, 6.0)
    return values.astype(jnp.bfloat16)


def draw_window_mask(key, part):
    key = jax.random.fold_in(key, 5)
    raw = jax.random.randint(key, (T_TILES, H_TILES, W_TILES, 27), 0, 4)
    centre = jnp.arange(27) == 13
    return jnp.where(centre, 1, jnp.minimum(raw, 1)).astype(jnp.int32)


def level_of(stream_key, extent, cuts, least, largest):
    def one(dim, shards_of):
        heights = jax.random.uniform(jax.random.fold_in(jax.random.fold_in(stream_key, 6), dim), (shards_of,), jnp.float32, least / len(cuts), largest / len(cuts))
        return jnp.repeat(jnp.exp(heights), extent[dim] // shards_of).reshape((-1,) + (1,) * (len(extent) - dim - 1))

    loudness = one(*cuts[0])
    for cut in cuts[1:]:
        loudness = loudness * one(*cut)
    return loudness


def scatter_about(rng, shape, spread, limit, split=(), kind=jnp.bfloat16):
    values = jax.random.normal(rng, shape, jnp.float32) * spread
    if len(split) > 0:
        values = level_of(rng, shape, split, -0.22, 0.18) * values
    return jnp.clip(values, min=-limit, max=limit).astype(kind)


def setup_inputs(seed: int = 0) -> dict:
    key_of = jax.random.split(jax.random.key(seed), 7)
    query_in = draw_query_in(jax.random.fold_in(key_of[6], 71), 0)
    key_in = draw_key_in(jax.random.fold_in(key_of[6], 71), 0)
    value_in = scatter_about(key_of[2], (FRAMES, PLANE_TILES, TILE_H, TILE_W, HD), 1.0, 6.0, ((0, 4), (1, 4), (4, 2)))
    saved_out = scatter_about(key_of[3], (FRAMES, PLANE_TILES, TILE_H, TILE_W, HD), 1.0, 6.0, ((0, 4), (1, 4), (4, 2)))
    out_grad = scatter_about(key_of[4], (FRAMES, PLANE_TILES, TILE_H, TILE_W, HD), 1.0, 6.0, ((0, 4), (1, 4), (4, 2)))
    window_mask = draw_window_mask(jax.random.fold_in(key_of[6], 71), 0)
    return {"query_in": query_in, "key_in": key_in, "value_in": value_in, "saved_out": saved_out, "out_grad": out_grad, "window_mask": window_mask}


def attend(query_rows, key_rows, value_rows, saved_rows, grad_rows, allowed, score_scale):
    f32 = jnp.float32
    scores = jnp.einsum("qhd,khd->hqk", query_rows.astype(f32), key_rows.astype(f32)) * score_scale
    scores = jnp.where(allowed[None, None, :], scores, -jnp.inf)
    row_max = jnp.max(scores, axis=-1, keepdims=True)
    raised = jnp.exp(scores - row_max)
    weights = raised / jnp.sum(raised, axis=-1, keepdims=True)
    weights_low = weights.astype(jnp.bfloat16)
    value_part = jnp.einsum("hqk,qhd->khd", weights_low.astype(f32), grad_rows.astype(f32)).astype(jnp.bfloat16)
    weight_grad = jnp.einsum("qhd,khd->hqk", grad_rows.astype(f32), value_rows.astype(f32))
    row_dot = jnp.einsum("qhd,qhd->hq", grad_rows.astype(f32), saved_rows.astype(f32))
    score_grad = (weights * (weight_grad - row_dot[:, :, None]) * score_scale).astype(jnp.bfloat16)
    query_part = jnp.einsum("hqk,khd->qhd", score_grad.astype(f32), key_rows.astype(f32)).astype(jnp.bfloat16)
    key_part = jnp.einsum("hqk,qhd->khd", score_grad.astype(f32), query_rows.astype(f32)).astype(jnp.bfloat16)
    return query_part, key_part, value_part


def reference(query_in, key_in, value_in, saved_out, out_grad, window_mask):
    score_scale = HEAD_DIM ** -0.5
    grid = (FRAMES, H_TILES, W_TILES, TILE_H, TILE_W, HD)
    pad_spec = ((0, 0), (1, 1), (1, 1), (0, 0), (0, 0), (0, 0))
    key_pad = jnp.pad(key_in.reshape(grid), pad_spec)
    value_pad = jnp.pad(value_in.reshape(grid), pad_spec)
    region = (FRAMES, 3, 3, TILE_H, TILE_W)
    frame_tile = jnp.broadcast_to((jnp.arange(FRAMES, dtype=jnp.int32) // TILE_T).reshape(-1, 1, 1, 1, 1), region).reshape(-1)
    row_step = jnp.broadcast_to((jnp.arange(3, dtype=jnp.int32) - 1).reshape(1, -1, 1, 1, 1), region).reshape(-1)
    col_step = jnp.broadcast_to((jnp.arange(3, dtype=jnp.int32) - 1).reshape(1, 1, -1, 1, 1), region).reshape(-1)
    zero = jnp.zeros((), jnp.int32)
    key_size = (FRAMES, 3, 3, TILE_H, TILE_W, HD)

    def step(carry, block):
        key_sum, value_sum = carry
        time_index = block // N_HA
        plane = block % N_HA
        row_tile = plane // W_TILES
        col_tile = plane % W_TILES
        query_time = (time_index * FRAMES_DEV) // TILE_T
        query_start = (time_index * FRAMES_DEV, plane, zero, zero, zero)
        query_size = (FRAMES_DEV, 1, TILE_H, TILE_W, HD)
        query_rows = lax.dynamic_slice(query_in, query_start, query_size).reshape(-1, HEADS, HEAD_DIM)
        saved_rows = lax.dynamic_slice(saved_out, query_start, query_size).reshape(-1, HEADS, HEAD_DIM)
        grad_rows = lax.dynamic_slice(out_grad, query_start, query_size).reshape(-1, HEADS, HEAD_DIM)
        key_start = (zero, row_tile, col_tile, zero, zero, zero)
        key_rows = lax.dynamic_slice(key_pad, key_start, key_size).reshape(-1, HEADS, HEAD_DIM)
        value_rows = lax.dynamic_slice(value_pad, key_start, key_size).reshape(-1, HEADS, HEAD_DIM)
        window_row = lax.dynamic_slice(window_mask, (query_time, row_tile, col_tile, zero), (1, 1, 1, 27)).reshape(27)
        code = (frame_tile - query_time + 1) * 9 + (row_step + 1) * 3 + (col_step + 1)
        picked = jnp.take(window_row, code.astype(jnp.int32))
        inside = (row_tile + row_step >= 0) & (row_tile + row_step < H_TILES)
        inside = inside & (col_tile + col_step >= 0) & (col_tile + col_step < W_TILES)
        allowed = (picked == 1) & inside
        query_part, key_part, value_part = attend(query_rows, key_rows, value_rows, saved_rows, grad_rows, allowed, score_scale)
        key_sum = lax.dynamic_update_slice(key_sum, lax.dynamic_slice(key_sum, key_start, key_size) + key_part.reshape(key_size).astype(jnp.float32), key_start)
        value_sum = lax.dynamic_update_slice(value_sum, lax.dynamic_slice(value_sum, key_start, key_size) + value_part.reshape(key_size).astype(jnp.float32), key_start)
        return (key_sum, value_sum), query_part.reshape(query_size)

    start_sums = (jnp.zeros(key_pad.shape, jnp.float32), jnp.zeros(key_pad.shape, jnp.float32))
    (key_sum, value_sum), query_blocks = lax.scan(step, start_sums, jnp.arange(N_TA * N_HA, dtype=jnp.int32))
    query_grad = query_blocks.reshape(N_TA, N_HA, FRAMES_DEV, TILE_H, TILE_W, HD).transpose(0, 2, 1, 3, 4, 5).reshape(FRAMES, PLANE_TILES, TILE_H, TILE_W, HD)
    out_shape = (FRAMES, PLANE_TILES, TILE_H, TILE_W, HD)
    key_grad = key_sum[:, 1:H_TILES + 1, 1:W_TILES + 1].reshape(out_shape).astype(jnp.bfloat16)
    value_grad = value_sum[:, 1:H_TILES + 1, 1:W_TILES + 1].reshape(out_shape).astype(jnp.bfloat16)
    return query_grad, key_grad, value_grad
```

```python
import functools

import jax
import jax.numpy as jnp
from jax import lax
from jax.experimental import pallas as pl
from jax.experimental.pallas import tpu as pltpu
from jax.sharding import PartitionSpec as P

HEAD_DIM = 128
TILE_T = 6
LOG2_E = 1.4426950408889634
LOWEST = -1e30
MESH = pl.DeviceIdType.MESH
KEY, QUERY, GRAD, VALUE = range(4)


def kernel(
    dims,
    mask_ref,
    q_ref,
    k_ref,
    v_ref,
    o_ref,
    g_ref,
    dq_ref,
    dk_ref,
    dv_ref,
    near,
    stats,
    raised,
    lifted_own,
    dq_acc,
    dk_acc,
    dv_acc,
    pair_sem,
    plane_sem,
    span_sem,
    recv_sem,
    stat_send,
    stat_recv,
):
    f32, bf16 = jnp.float32, jnp.bfloat16
    n_ta, row_tiles, col_tiles, frames_dev, heads, moves = dims
    rows = q_ref.shape[0]
    n_slot = len(moves)
    centre = moves.index((0, 0))
    others = [s for s in range(n_slot) if s != centre]
    order = [centre] + others
    keys = n_ta * rows
    scale = HEAD_DIM ** (-0.5)
    to_two = scale * LOG2_E
    n_low = 2 if n_ta % 2 == 0 else 1
    n_high = n_ta // n_low

    time = lax.axis_index("ta")
    plane = lax.axis_index("ha")
    group = lax.axis_index("ga")
    high, low = time // n_low, time % n_low
    row_tile = plane // col_tiles
    col_tile = plane % col_tiles
    inside = [
        (row_tile + dr >= 0)
        & (row_tile + dr < row_tiles)
        & (col_tile + dc >= 0)
        & (col_tile + dc < col_tiles)
        for dr, dc in moves
    ]
    own = {KEY: k_ref, QUERY: q_ref, GRAD: g_ref, VALUE: v_ref}

    def shifted(s):
        dr, dc = moves[s]
        return plane + dr * col_tiles + dc

    def back(s):
        return n_slot - 1 - s

    def if_inside(s, do):
        if s == centre:
            do()
        else:
            pl.when(inside[s])(do)

    def push(src, a, s, j, send_sem, device):
        return pltpu.make_async_remote_copy(
            src_ref=src,
            dst_ref=near.at[a, s, j],
            send_sem=send_sem,
            recv_sem=recv_sem.at[a, s, j],
            device_id=device,
            device_id_type=MESH,
        )

    def held(a, s, d):
        if s == centre and d == 0:
            return own[a], time
        j = (high + d) % n_high * n_low + low
        return near.at[a, s, j], j

    def span_copy(a, d):
        j = (high + d) % n_high * n_low + low
        return push(own[a], a, centre, time, span_sem.at[a, d], (j, plane, group))

    def plane_copy(a, s, d):
        src, j = held(a, centre, d)
        return push(src, a, back(s), j, plane_sem.at[a, s, d], (time, shifted(s), group))

    def pair_copy(a, s, d):
        src, j = held(a, s, d)
        partner = high * n_low + 1 - low
        return push(src, a, s, j, pair_sem.at[a, s, d], (partner, plane, group))

    def arrived(a, s, j):
        block = near.at[a, s, j]
        push(block, a, s, j, recv_sem.at[a, s, j], (time, plane, group)).wait_recv()

    def wait_chain(a, s):
        for d in range(n_high):
            if s != centre or d != 0:
                arrived(a, s, (high + d) % n_high * n_low + low)

    def wait_pair(a, s):
        if n_low == 2:
            for h in range(n_high):
                arrived(a, s, h * n_low + 1 - low)

    def start_pair(a, s, d):
        if n_low == 2:
            pair_copy(a, s, d).start()

    def start_planes(a, d):
        for s in others:
            if_inside(s, lambda s=s: plane_copy(a, s, d).start())

    def pass_on_span(a):
        wait_chain(a, centre)
        for d in range(1, n_high):
            start_planes(a, d)
            start_pair(a, centre, d)

    def pass_on_planes(a):
        for s in others:

            def do(s=s):
                wait_chain(a, s)
                for d in range(n_high):
                    start_pair(a, s, d)

            if_inside(s, do)

    def wait_rest(a, s):
        if_inside(s, lambda: wait_pair(a, s))

    def stat_copy(s, j):
        return pltpu.make_async_remote_copy(
            src_ref=stats.at[centre, time],
            dst_ref=stats.at[back(s), time],
            send_sem=stat_send.at[s, j],
            recv_sem=stat_recv.at[back(s), time],
            device_id=(j, shifted(s), group),
            device_id_type=MESH,
        )

    def stat_arrived(s, j):
        block = stats.at[s, j]
        pltpu.make_async_remote_copy(
            src_ref=block,
            dst_ref=block,
            send_sem=stat_send.at[s, j],
            recv_sem=stat_recv.at[s, j],
            device_id=(time, plane, group),
            device_id_type=MESH,
        ).wait_recv()

    def each_peer(s, do):
        for j in range(n_ta):
            if s == centre:
                pl.when(time != j)(functools.partial(do, s, j))
            else:
                pl.when(inside[s])(functools.partial(do, s, j))

    barrier = pltpu.get_barrier_semaphore()

    def greet(s, j):
        pl.semaphore_signal(
            barrier, inc=1, device_id=(j, shifted(s), group), device_id_type=MESH
        )

    for s in order:
        each_peer(s, greet)
    planes = sum(jnp.where(inside[s], 1, 0) for s in range(n_slot))
    pl.semaphore_wait(barrier, planes * n_ta - 1)

    for a in (KEY, QUERY, GRAD, VALUE):
        for d in range(1, n_high):
            span_copy(a, d).start()
        if a == KEY:
            start_planes(a, 0)
    for a in (KEY, QUERY, GRAD, VALUE):
        start_pair(a, centre, 0)

    for a in (KEY, QUERY, GRAD, VALUE):
        near[a, centre, time] = own[a][...]
    for s in others:

        @pl.when(jnp.logical_not(inside[s]))
        def _(s=s):
            for a in (KEY, QUERY, GRAD, VALUE):
                near[a, s] = jnp.zeros(near.shape[2:], bf16)
            stats[s] = jnp.zeros(stats.shape[1:], f32)

    head_of = [slice(h * HEAD_DIM, (h + 1) * HEAD_DIM) for h in range(heads)]
    column = lax.broadcasted_iota(jnp.int32, (1, keys), 1)
    row_dot = [
        jnp.sum(
            g_ref[:, head_of[h]].astype(f32) * o_ref[:, head_of[h]].astype(f32),
            axis=-1,
            keepdims=True,
        )
        * scale
        for h in range(heads)
    ]

    def tile_time(j):
        return j * frames_dev // TILE_T

    def open_bias(s, as_query):
        dr, dc = moves[s]
        bias = jnp.full((1, keys), -jnp.inf, f32)
        for j in range(n_ta):
            if as_query:
                query_time, time_step = tile_time(time), tile_time(j) - tile_time(time)
                query_row, query_col, row_step, col_step = row_tile, col_tile, dr, dc
            else:
                query_time, time_step = tile_time(j), tile_time(time) - tile_time(j)
                query_row = jnp.clip(row_tile + dr, 0, row_tiles - 1)
                query_col = jnp.clip(col_tile + dc, 0, col_tiles - 1)
                row_step, col_step = -dr, -dc
            close = (time_step >= -1) & (time_step <= 1)
            code = (jnp.clip(time_step, -1, 1) + 1) * 9 + (row_step + 1) * 3 + (col_step + 1)
            tile = (query_time * row_tiles + query_row) * col_tiles + query_col
            is_open = (mask_ref[tile * 27 + code] == 1) & close & inside[s]
            here = (column >= j * rows) & (column < (j + 1) * rows)
            bias = jnp.where(here & is_open, 0.0, bias)
        return bias

    def dot(a, b, dims):
        return lax.dot_general(a, b, (dims, ((), ())), preferred_element_type=f32)

    def block_of(a, s, h):
        return near[a, s, :, :, head_of[h]].reshape(keys, HEAD_DIM)

    slot_max = {}
    slot_sum = {}

    def own_scores(s):
        bias = open_bias(s, True)
        for h in range(heads):
            scores = dot(q_ref[:, head_of[h]], block_of(KEY, s, h), ((1,), (1,))) + bias
            top = jnp.maximum(jnp.max(scores, axis=-1, keepdims=True), LOWEST)
            lifted = jnp.exp2((scores - top) * to_two)
            raised[s, h] = lifted
            slot_max[s, h] = top
            slot_sum[s, h] = jnp.sum(lifted, axis=-1, keepdims=True)

    pass_on_span(KEY)
    start_planes(QUERY, 0)
    wait_rest(KEY, centre)
    own_scores(centre)
    pass_on_span(QUERY)
    pass_on_planes(KEY)
    start_planes(GRAD, 0)
    for s in others:
        wait_rest(KEY, s)
        own_scores(s)
    pass_on_span(GRAD)
    start_planes(VALUE, 0)

    factor = {}
    columns = []
    for h in range(heads):
        top = slot_max[centre, h]
        for s in others:
            top = jnp.maximum(top, slot_max[s, h])
        gain = {s: jnp.exp2((slot_max[s, h] - top) * to_two) for s in order}
        total = gain[centre] * slot_sum[centre, h]
        for s in others:
            total = total + gain[s] * slot_sum[s, h]
        for s in order:
            factor[s, h] = gain[s] / total
        columns.append(top * to_two + jnp.log2(total))
    columns = columns + row_dot
    lane = lax.broadcasted_iota(jnp.int32, (rows, HEAD_DIM), 1)
    table = jnp.zeros((rows, HEAD_DIM), f32)
    for index, col in enumerate(columns):
        table = jnp.where(lane == index, col, table)
    stats[centre, time] = table.T[: stats.shape[2]]
    for s in order:
        each_peer(s, lambda s, j: stat_copy(s, j).start())
    pass_on_span(VALUE)

    def stat_rows(s):
        return jnp.concatenate([stats[s, j] for j in range(n_ta)], axis=1)

    def key_weights(s):
        each_peer(s, stat_arrived)
        bias = open_bias(s, False)
        table = stat_rows(s)
        for h in range(heads):
            scores = dot(k_ref[:, head_of[h]], block_of(QUERY, s, h), ((1,), (1,)))
            lifted_own[s, h] = jnp.exp2(scores * to_two + (bias - table[h : h + 1]))

    def add(acc, h, first, part):
        if first:
            acc[:, head_of[h]] = part
        else:
            acc[:, head_of[h]] += part

    def key_grads(s):
        table = stat_rows(s)
        for h in range(heads):
            grads = block_of(GRAD, s, h)
            weights = lifted_own[s, h]
            add(dv_acc, h, s == centre, dot(weights.astype(bf16), grads, ((1,), (0,))))
            weight_grad = dot(v_ref[:, head_of[h]], grads, ((1,), (1,)))
            shift = table[heads + h : heads + h + 1]
            score_grad = (weights * (weight_grad * scale - shift)).astype(bf16)
            part = dot(score_grad, block_of(QUERY, s, h), ((1,), (0,)))
            add(dk_acc, h, s == centre, part)

    def query_grads(s):
        for h in range(heads):
            weight_grad = dot(g_ref[:, head_of[h]], block_of(VALUE, s, h), ((1,), (1,)))
            weights = raised[s, h] * factor[s, h]
            score_grad = (weights * (weight_grad * scale - row_dot[h])).astype(bf16)
            part = dot(score_grad, block_of(KEY, s, h), ((1,), (0,)))
            add(dq_acc, h, s == centre, part)

    pass_on_planes(QUERY)
    for s in order:
        wait_rest(QUERY, s)
        key_weights(s)
    wait_rest(GRAD, centre)
    key_grads(centre)
    wait_rest(VALUE, centre)
    query_grads(centre)
    pass_on_planes(GRAD)
    for s in others:
        wait_rest(GRAD, s)
        key_grads(s)
    pass_on_planes(VALUE)
    dk_ref[...] = dk_acc[...].astype(bf16)
    dv_ref[...] = dv_acc[...].astype(bf16)
    for s in others:
        wait_rest(VALUE, s)
        query_grads(s)
    dq_ref[...] = dq_acc[...].astype(bf16)

    for a in (KEY, QUERY, GRAD, VALUE):
        for d in range(1, n_high):
            span_copy(a, d).wait_send()
        for s in order:

            def finish(s=s, a=a):
                for d in range(n_high):
                    if s != centre:
                        plane_copy(a, s, d).wait_send()
                    if n_low == 2:
                        pair_copy(a, s, d).wait_send()

            if_inside(s, finish)
    for s in order:
        each_peer(s, lambda s, j: stat_copy(s, j).wait_send())


def local(n_ta, query_in, key_in, value_in, saved_out, out_grad, window_mask):
    f32, bf16 = jnp.float32, jnp.bfloat16
    shape = query_in.shape
    frames_dev, _, tile_rows, tile_cols, width = shape
    rows = frames_dev * tile_rows * tile_cols
    heads = width // HEAD_DIM
    _, row_tiles, col_tiles, _ = window_mask.shape
    moves = [
        (dr, dc)
        for dr in (-1, 0, 1)
        for dc in (-1, 0, 1)
        if abs(dr) < row_tiles and abs(dc) < col_tiles
    ]
    n_slot = len(moves)
    dims = (n_ta, row_tiles, col_tiles, frames_dev, heads, moves)
    vmem = pl.BlockSpec(memory_space=pltpu.VMEM)
    out = jax.ShapeDtypeStruct((rows, width), bf16)
    stat_rows = -(-2 * heads // 8) * 8
    weights = pltpu.VMEM((n_slot, heads, rows, n_ta * rows), f32)
    total = pltpu.VMEM((rows, width), f32)
    dma = pltpu.SemaphoreType.DMA
    results = pl.pallas_call(
        functools.partial(kernel, dims),
        out_shape=(out, out, out),
        in_specs=[pl.BlockSpec(memory_space=pltpu.SMEM)] + [vmem] * 5,
        out_specs=(vmem, vmem, vmem),
        scratch_shapes=[
            pltpu.VMEM((4, n_slot, n_ta, rows, width), bf16),
            pltpu.VMEM((n_slot, n_ta, stat_rows, rows), f32),
            weights,
            weights,
            total,
            total,
            total,
            dma((4, n_slot, n_ta)),
            dma((4, n_slot, n_ta)),
            dma((4, n_ta)),
            dma((4, n_slot, n_ta)),
            dma((n_slot, n_ta)),
            dma((n_slot, n_ta)),
        ],
        compiler_params=pltpu.CompilerParams(
            collective_id=0, has_side_effects=True, vmem_limit_bytes=56 * 1024 * 1024
        ),
    )(
        window_mask.reshape(-1),
        *(x.reshape(rows, width) for x in (query_in, key_in, value_in, saved_out, out_grad)),
    )
    return tuple(x.reshape(shape) for x in results)


def solution(mesh):
    spec = P("ta", "ha", None, None, "ga")
    return jax.shard_map(
        functools.partial(local, mesh.shape["ta"]),
        mesh=mesh,
        in_specs=(spec, spec, spec, spec, spec, P()),
        out_specs=(spec, spec, spec),
        check_vma=False,
    )
```

```python
import functools

import jax
import jax.numpy as jnp
from jax import lax
from jax.experimental import pallas as pl
from jax.experimental.pallas import tpu as pltpu
from jax.sharding import PartitionSpec as P

HEAD_DIM = 128
TILE_T = 6
LOG2_E = 1.4426950408889634
LOWEST = -1e30
MESH = pl.DeviceIdType.MESH
KEY, QUERY, GRAD, VALUE = range(4)
ACROSS_SPAN = (QUERY,)


def kernel(
    dims,
    mask_ref,
    q_ref,
    k_ref,
    v_ref,
    o_ref,
    g_ref,
    dq_ref,
    dk_ref,
    dv_ref,
    near,
    stats,
    raised,
    lifted_own,
    dq_acc,
    dk_acc,
    dv_acc,
    saved,
    load_sem,
    pair_sem,
    plane_sem,
    span_sem,
    recv_sem,
    stat_send,
    stat_recv,
):
    f32, bf16 = jnp.float32, jnp.bfloat16
    n_ta, row_tiles, col_tiles, frames_dev, heads, moves = dims
    rows = saved.shape[0]
    n_slot = len(moves)
    centre = moves.index((0, 0))
    others = [s for s in range(n_slot) if s != centre]
    order = [centre] + others
    keys = n_ta * rows
    step = 256 if keys % 256 == 0 else keys
    chunks = [slice(at, at + step) for at in range(0, keys, step)]
    scale = HEAD_DIM ** (-0.5)
    to_two = scale * LOG2_E
    n_low = 2 if n_ta % 2 == 0 else 1
    n_high = n_ta // n_low

    time = lax.axis_index("ta")
    plane = lax.axis_index("ha")
    group = lax.axis_index("ga")
    high, low = time // n_low, time % n_low
    row_tile = plane // col_tiles
    col_tile = plane % col_tiles
    inside = [
        (row_tile + dr >= 0)
        & (row_tile + dr < row_tiles)
        & (col_tile + dc >= 0)
        & (col_tile + dc < col_tiles)
        for dr, dc in moves
    ]
    own = {KEY: k_ref, QUERY: q_ref, GRAD: g_ref, VALUE: v_ref}

    def shifted(s):
        dr, dc = moves[s]
        return plane + dr * col_tiles + dc

    def back(s):
        return n_slot - 1 - s

    def if_inside(s, do):
        if s == centre:
            do()
        else:
            pl.when(inside[s])(do)

    def push(src, a, s, j, send_sem, device):
        return pltpu.make_async_remote_copy(
            src_ref=src,
            dst_ref=near.at[a, s, j],
            send_sem=send_sem,
            recv_sem=recv_sem.at[a, s, j],
            device_id=device,
            device_id_type=MESH,
        )

    def held(a, s, d):
        if s == centre and d == 0:
            return own[a], time
        j = (high + d) % n_high * n_low + low
        return near.at[a, s, j], j

    def span_copy(a, s, d):
        src, _ = held(a, s, 0)
        j = (high + d) % n_high * n_low + low
        return push(src, a, s, time, span_sem.at[a, s, d], (j, plane, group))

    def start_span(a, s):
        for d in range(1, n_high):
            span_copy(a, s, d).start()

    def plane_copy(a, s, d):
        src, j = held(a, centre, d)
        return push(src, a, back(s), j, plane_sem.at[a, s, d], (time, shifted(s), group))

    def pair_copy(a, s, d):
        src, j = held(a, s, d)
        partner = high * n_low + 1 - low
        return push(src, a, s, j, pair_sem.at[a, s, d], (partner, plane, group))

    def arrived(a, s, j):
        block = near.at[a, s, j]
        push(block, a, s, j, recv_sem.at[a, s, j], (time, plane, group)).wait_recv()

    def chain_arrived(a, s, d):
        arrived(a, s, (high + d) % n_high * n_low + low)

    def wait_pair(a, s):
        if n_low == 2:
            for h in range(n_high):
                arrived(a, s, h * n_low + 1 - low)

    def start_pair(a, s, d):
        if n_low == 2:
            pair_copy(a, s, d).start()

    def start_planes(a, d):
        for s in others:
            if_inside(s, lambda s=s: plane_copy(a, s, d).start())

    def pass_on_span(a):
        for d in range(1, n_high):
            chain_arrived(a, centre, d)
            if a not in ACROSS_SPAN:
                start_planes(a, d)
            start_pair(a, centre, d)

    def pass_on_planes(a, s, d):
        def do():
            chain_arrived(a, s, d)
            if a in ACROSS_SPAN and d == 0:
                start_span(a, s)
            start_pair(a, s, d)

        if_inside(s, do)

    def wait_rest(a, s):
        if_inside(s, lambda: wait_pair(a, s))

    def stat_copy(s, j):
        return pltpu.make_async_remote_copy(
            src_ref=stats.at[centre, time],
            dst_ref=stats.at[back(s), time],
            send_sem=stat_send.at[s, j],
            recv_sem=stat_recv.at[back(s), time],
            device_id=(j, shifted(s), group),
            device_id_type=MESH,
        )

    def stat_arrived(s, j):
        block = stats.at[s, j]
        pltpu.make_async_remote_copy(
            src_ref=block,
            dst_ref=block,
            send_sem=stat_send.at[s, j],
            recv_sem=stat_recv.at[s, j],
            device_id=(time, plane, group),
            device_id_type=MESH,
        ).wait_recv()

    def each_peer(s, do):
        for j in range(n_ta):
            if s == centre:
                pl.when(time != j)(functools.partial(do, s, j))
            else:
                pl.when(inside[s])(functools.partial(do, s, j))

    loads = [
        pltpu.make_async_copy(own[a], near.at[a, centre, time], load_sem.at[a])
        for a in (KEY, QUERY, GRAD, VALUE)
    ] + [pltpu.make_async_copy(o_ref, saved, load_sem.at[4])]
    for load in loads:
        load.start()

    barrier = pltpu.get_barrier_semaphore()

    def greet(s, j):
        pl.semaphore_signal(
            barrier, inc=1, device_id=(j, shifted(s), group), device_id_type=MESH
        )

    for s in order:
        each_peer(s, greet)
    planes = sum(jnp.where(inside[s], 1, 0) for s in range(n_slot))
    pl.semaphore_wait(barrier, planes * n_ta - 1)

    start_planes(KEY, 0)
    for a in (KEY, VALUE, QUERY, GRAD):
        start_span(a, centre)
        start_pair(a, centre, 0)

    for s in others:

        @pl.when(jnp.logical_not(inside[s]))
        def _(s=s):
            for a in (KEY, QUERY, GRAD, VALUE):
                near[a, s] = jnp.zeros(near.shape[2:], bf16)
            stats[s] = jnp.zeros(stats.shape[1:], f32)

    for load in loads:
        load.wait()

    head_of = [slice(h * HEAD_DIM, (h + 1) * HEAD_DIM) for h in range(heads)]
    column = lax.broadcasted_iota(jnp.int32, (1, keys), 1)
    def mine(a, h):
        return near[a, centre, time, :, head_of[h]]

    row_dot = [
        jnp.sum(
            mine(GRAD, h).astype(f32) * saved[:, head_of[h]].astype(f32),
            axis=-1,
            keepdims=True,
        )
        for h in range(heads)
    ]

    def tile_time(j):
        return j * frames_dev // TILE_T

    def open_bias(s, as_query):
        dr, dc = moves[s]
        bias = jnp.full((1, keys), -jnp.inf, f32)
        for j in range(n_ta):
            if as_query:
                query_time, time_step = tile_time(time), tile_time(j) - tile_time(time)
                query_row, query_col, row_step, col_step = row_tile, col_tile, dr, dc
            else:
                query_time, time_step = tile_time(j), tile_time(time) - tile_time(j)
                query_row = jnp.clip(row_tile + dr, 0, row_tiles - 1)
                query_col = jnp.clip(col_tile + dc, 0, col_tiles - 1)
                row_step, col_step = -dr, -dc
            close = (time_step >= -1) & (time_step <= 1)
            code = (jnp.clip(time_step, -1, 1) + 1) * 9 + (row_step + 1) * 3 + (col_step + 1)
            is_open = (mask_ref[query_time, query_row, query_col, code] == 1) & close & inside[s]
            here = (column >= j * rows) & (column < (j + 1) * rows)
            bias = jnp.where(here & is_open, 0.0, bias)
        return bias

    def dot(a, b, dims):
        return lax.dot_general(a, b, (dims, ((), ())), preferred_element_type=f32)

    def block_of(a, s, h):
        return near[a, s, :, :, head_of[h]].reshape(keys, HEAD_DIM)

    slot_max = {}
    slot_sum = {}

    def fold(values, combine):
        parts = [values[:, at : at + 128] for at in range(0, step, 128)]
        return functools.reduce(combine, parts)

    def own_scores(s):
        bias = open_bias(s, True)
        for h in range(heads):
            query, near_keys = mine(QUERY, h), block_of(KEY, s, h)
            tops = []
            for c in chunks:
                scores = dot(query, near_keys[c], ((1,), (1,))) + bias[:, c]
                raised[s, h, :, c] = scores
                tops.append(fold(scores, jnp.maximum))
            top = functools.reduce(jnp.maximum, tops)
            top = jnp.maximum(jnp.max(top, axis=-1, keepdims=True), LOWEST)
            sums = []
            for c in chunks:
                lifted = jnp.exp2((raised[s, h, :, c] - top) * to_two)
                raised[s, h, :, c] = lifted
                sums.append(fold(lifted, jnp.add))
            total = functools.reduce(jnp.add, sums)
            slot_max[s, h] = top
            slot_sum[s, h] = jnp.sum(total, axis=-1, keepdims=True)

    pass_on_span(KEY)
    start_planes(VALUE, 0)
    start_planes(QUERY, 0)
    wait_rest(KEY, centre)
    own_scores(centre)
    pass_on_span(VALUE)
    start_planes(GRAD, 0)
    for s in others:
        for d in range(n_high):
            pass_on_planes(KEY, s, d)
    for s in others:
        wait_rest(KEY, s)
        own_scores(s)

    factor = {}
    columns = []
    for h in range(heads):
        top = slot_max[centre, h]
        for s in others:
            top = jnp.maximum(top, slot_max[s, h])
        gain = {s: jnp.exp2((slot_max[s, h] - top) * to_two) for s in order}
        total = gain[centre] * slot_sum[centre, h]
        for s in others:
            total = total + gain[s] * slot_sum[s, h]
        for s in order:
            factor[s, h] = gain[s] * (scale / total)
        columns.append(top * to_two + jnp.log2(total))
    columns = columns + row_dot
    lane = lax.broadcasted_iota(jnp.int32, (rows, HEAD_DIM), 1)
    table = jnp.zeros((rows, HEAD_DIM), f32)
    for index, col in enumerate(columns):
        table = jnp.where(lane == index, col, table)
    stats[centre, time] = table.T[: stats.shape[2]]
    for s in order:
        each_peer(s, lambda s, j: stat_copy(s, j).start())

    def stat_rows(s):
        return jnp.concatenate([stats[s, j] for j in range(n_ta)], axis=1)

    def key_weights(s):
        each_peer(s, stat_arrived)
        bias = open_bias(s, False)
        table = stat_rows(s)
        for h in range(heads):
            key, queries = mine(KEY, h), block_of(QUERY, s, h)
            shift = bias - table[h : h + 1]
            for c in chunks:
                scores = dot(key, queries[c], ((1,), (1,)))
                lifted_own[s, h, :, c] = jnp.exp2(scores * to_two + shift[:, c])

    def add(acc, h, first, part):
        if first:
            acc[:, head_of[h]] = part
        else:
            acc[:, head_of[h]] += part

    def key_grads(s):
        table = stat_rows(s)
        for h in range(heads):
            grads, queries, value = block_of(GRAD, s, h), block_of(QUERY, s, h), mine(VALUE, h)
            shift = table[heads + h : heads + h + 1]
            value_part = key_part = 0.0
            for c in chunks:
                weights = lifted_own[s, h, :, c]
                value_part += dot(weights.astype(bf16), grads[c], ((1,), (0,)))
                weight_grad = dot(value, grads[c], ((1,), (1,)))
                score_grad = (weights * (weight_grad - shift[:, c])).astype(bf16)
                key_part += dot(score_grad, queries[c], ((1,), (0,)))
            add(dv_acc, h, s == centre, value_part)
            add(dk_acc, h, s == centre, key_part)

    def query_grads(s):
        for h in range(heads):
            grad, values, near_keys = mine(GRAD, h), block_of(VALUE, s, h), block_of(KEY, s, h)
            query_part = 0.0
            for c in chunks:
                weight_grad = dot(grad, values[c], ((1,), (1,)))
                score_grad = (raised[s, h, :, c] * (weight_grad - row_dot[h])).astype(bf16)
                query_part += dot(score_grad, near_keys[c], ((1,), (0,)))
            add(dq_acc, h, s == centre, query_part * factor[s, h])

    pass_on_span(QUERY)
    pass_on_span(GRAD)
    wait_rest(VALUE, centre)
    query_grads(centre)
    for a in (VALUE, QUERY):
        for s in others:
            pass_on_planes(a, s, 0)
    wait_rest(QUERY, centre)
    key_weights(centre)
    wait_rest(GRAD, centre)
    key_grads(centre)
    for s in others:
        for d in range(1, n_high):
            pass_on_planes(VALUE, s, d)
    for s in others:
        wait_rest(VALUE, s)
        query_grads(s)
    dq_ref[...] = dq_acc[...].astype(bf16)
    for s in others:
        pass_on_planes(GRAD, s, 0)
        for d in range(1, n_high):
            pass_on_planes(QUERY, s, d)
    for s in others:
        wait_rest(QUERY, s)
        key_weights(s)
    for s in others:
        for d in range(1, n_high):
            pass_on_planes(GRAD, s, d)
    for s in others:
        wait_rest(GRAD, s)
        key_grads(s)
    dk_ref[...] = (dk_acc[...] * scale).astype(bf16)
    dv_ref[...] = dv_acc[...].astype(bf16)

    for a in (KEY, QUERY, GRAD, VALUE):
        for s in order:

            def finish(s=s, a=a):
                for d in range(n_high):
                    if s != centre and (d == 0 or a not in ACROSS_SPAN):
                        plane_copy(a, s, d).wait_send()
                    if d != 0 and (s == centre or a in ACROSS_SPAN):
                        span_copy(a, s, d).wait_send()
                    if n_low == 2:
                        pair_copy(a, s, d).wait_send()

            if_inside(s, finish)
    for s in order:
        each_peer(s, lambda s, j: stat_copy(s, j).wait_send())


def write_results(dq_ref, dk_ref, dv_ref, query_grad, key_grad, value_grad):
    query_grad[...] = dq_ref[...]
    key_grad[...] = dk_ref[...]
    value_grad[...] = dv_ref[...]


def local(n_ta, query_in, key_in, value_in, saved_out, out_grad, window_mask):
    f32, bf16 = jnp.float32, jnp.bfloat16
    shape = query_in.shape
    frames_dev, _, tile_rows, tile_cols, width = shape
    rows = frames_dev * tile_rows * tile_cols
    heads = width // HEAD_DIM
    _, row_tiles, col_tiles, _ = window_mask.shape
    moves = [
        (dr, dc)
        for dr in (-1, 0, 1)
        for dc in (-1, 0, 1)
        if abs(dr) < row_tiles and abs(dc) < col_tiles
    ]
    n_slot = len(moves)
    dims = (n_ta, row_tiles, col_tiles, frames_dev, heads, moves)
    vmem = pl.BlockSpec(memory_space=pltpu.VMEM)
    out = jax.ShapeDtypeStruct((rows, width), bf16)
    stat_rows = -(-2 * heads // 8) * 8
    weights = pltpu.VMEM((n_slot, heads, rows, n_ta * rows), f32)
    total = pltpu.VMEM((rows, width), f32)
    dma = pltpu.SemaphoreType.DMA
    kept = pl.BlockSpec(memory_space=pl.ANY)
    results = pl.pallas_call(
        functools.partial(kernel, dims),
        out_shape=(out, out, out),
        in_specs=[pl.BlockSpec(memory_space=pltpu.SMEM)] + [kept] * 5,
        out_specs=(vmem, vmem, vmem),
        scratch_shapes=[
            pltpu.VMEM((4, n_slot, n_ta, rows, width), bf16),
            pltpu.VMEM((n_slot, n_ta, stat_rows, rows), f32),
            weights,
            weights,
            total,
            total,
            total,
            pltpu.VMEM((rows, width), bf16),
            dma((5,)),
            dma((4, n_slot, n_ta)),
            dma((4, n_slot, n_ta)),
            dma((4, n_slot, n_ta)),
            dma((4, n_slot, n_ta)),
            dma((n_slot, n_ta)),
            dma((n_slot, n_ta)),
        ],
        compiler_params=pltpu.CompilerParams(
            collective_id=0, has_side_effects=True, vmem_limit_bytes=56 * 1024 * 1024
        ),
    )(
        window_mask,
        *(x.reshape(rows, width) for x in (query_in, key_in, value_in, saved_out, out_grad)),
    )
    results = pl.pallas_call(
        write_results,
        out_shape=(out, out, out),
        in_specs=[vmem] * 3,
        out_specs=(vmem, vmem, vmem),
    )(*results)
    return tuple(x.reshape(shape) for x in results)


def solution(mesh):
    spec = P("ta", "ha", None, None, "ga")
    return jax.shard_map(
        functools.partial(local, mesh.shape["ta"]),
        mesh=mesh,
        in_specs=(spec, spec, spec, spec, spec, P()),
        out_specs=(spec, spec, spec),
        check_vma=False,
    )
```

```python
import functools

import jax
import jax.numpy as jnp
from jax import lax
from jax.experimental import pallas as pl
from jax.experimental.pallas import tpu as pltpu
from jax.sharding import PartitionSpec as P

HEAD_DIM = 128
TILE_T = 6
LOG2_E = 1.4426950408889634
LOWEST = -1e30
MESH = pl.DeviceIdType.MESH
KEY, QUERY, GRAD, VALUE = range(4)
ACROSS_SPAN = (QUERY,)


def kernel(
    dims,
    mask_ref,
    q_ref,
    k_ref,
    v_ref,
    o_ref,
    g_ref,
    dq_ref,
    dk_ref,
    dv_ref,
    near,
    stats,
    raised,
    lifted_own,
    dq_acc,
    dk_acc,
    dv_acc,
    saved,
    load_sem,
    pair_sem,
    plane_sem,
    span_sem,
    recv_sem,
    stat_send,
    stat_recv,
):
    f32, bf16 = jnp.float32, jnp.bfloat16
    n_ta, row_tiles, col_tiles, frames_dev, heads, moves = dims
    rows = saved.shape[0]
    n_slot = len(moves)
    centre = moves.index((0, 0))
    others = [s for s in range(n_slot) if s != centre]
    order = [centre] + others
    keys = n_ta * rows
    step = 256 if keys % 256 == 0 else keys
    chunks = [slice(at, at + step) for at in range(0, keys, step)]
    scale = HEAD_DIM ** (-0.5)
    to_two = scale * LOG2_E
    n_low = 2 if n_ta % 2 == 0 else 1
    n_high = n_ta // n_low

    time = lax.axis_index("ta")
    plane = lax.axis_index("ha")
    group = lax.axis_index("ga")
    high, low = time // n_low, time % n_low
    row_tile = plane // col_tiles
    col_tile = plane % col_tiles
    inside = [
        (row_tile + dr >= 0)
        & (row_tile + dr < row_tiles)
        & (col_tile + dc >= 0)
        & (col_tile + dc < col_tiles)
        for dr, dc in moves
    ]
    own = {KEY: k_ref, QUERY: q_ref, GRAD: g_ref, VALUE: v_ref}

    def shifted(s):
        dr, dc = moves[s]
        return plane + dr * col_tiles + dc

    def back(s):
        return n_slot - 1 - s

    def if_inside(s, do):
        if s == centre:
            do()
        else:
            pl.when(inside[s])(do)

    def push(src, a, s, j, send_sem, device):
        return pltpu.make_async_remote_copy(
            src_ref=src,
            dst_ref=near.at[a, s, j],
            send_sem=send_sem,
            recv_sem=recv_sem.at[a, s, j],
            device_id=device,
            device_id_type=MESH,
        )

    def held(a, s, d):
        if s == centre and d == 0:
            return own[a], time
        j = (high + d) % n_high * n_low + low
        return near.at[a, s, j], j

    def span_copy(a, s, d):
        src, _ = held(a, s, 0)
        j = (high + d) % n_high * n_low + low
        return push(src, a, s, time, span_sem.at[a, s, d], (j, plane, group))

    def start_span(a, s):
        for d in range(1, n_high):
            span_copy(a, s, d).start()

    def plane_copy(a, s, d):
        src, j = held(a, centre, d)
        return push(src, a, back(s), j, plane_sem.at[a, s, d], (time, shifted(s), group))

    def pair_copy(a, s, d):
        src, j = held(a, s, d)
        partner = high * n_low + 1 - low
        return push(src, a, s, j, pair_sem.at[a, s, d], (partner, plane, group))

    def arrived(a, s, j):
        block = near.at[a, s, j]
        push(block, a, s, j, recv_sem.at[a, s, j], (time, plane, group)).wait_recv()

    def chain_arrived(a, s, d):
        arrived(a, s, (high + d) % n_high * n_low + low)

    def wait_pair(a, s):
        if n_low == 2:
            for h in range(n_high):
                arrived(a, s, h * n_low + 1 - low)

    def start_pair(a, s, d):
        if n_low == 2:
            pair_copy(a, s, d).start()

    def start_planes(a, d):
        for s in others:
            if_inside(s, lambda s=s: plane_copy(a, s, d).start())

    def pass_on_span(a):
        for d in range(1, n_high):
            chain_arrived(a, centre, d)
            if a not in ACROSS_SPAN:
                start_planes(a, d)
            start_pair(a, centre, d)

    def pass_on_planes(a, s, d):
        def do():
            chain_arrived(a, s, d)
            if a in ACROSS_SPAN and d == 0:
                start_span(a, s)
            start_pair(a, s, d)

        if_inside(s, do)

    def wait_rest(a, s):
        if_inside(s, lambda: wait_pair(a, s))

    def stat_copy(s, j):
        return pltpu.make_async_remote_copy(
            src_ref=stats.at[centre, time],
            dst_ref=stats.at[back(s), time],
            send_sem=stat_send.at[s, j],
            recv_sem=stat_recv.at[back(s), time],
            device_id=(j, shifted(s), group),
            device_id_type=MESH,
        )

    def stat_arrived(s, j):
        block = stats.at[s, j]
        pltpu.make_async_remote_copy(
            src_ref=block,
            dst_ref=block,
            send_sem=stat_send.at[s, j],
            recv_sem=stat_recv.at[s, j],
            device_id=(time, plane, group),
            device_id_type=MESH,
        ).wait_recv()

    def each_peer(s, do):
        for j in range(n_ta):
            if s == centre:
                pl.when(time != j)(functools.partial(do, s, j))
            else:
                pl.when(inside[s])(functools.partial(do, s, j))

    loads = [
        pltpu.make_async_copy(own[a], near.at[a, centre, time], load_sem.at[a])
        for a in (KEY, QUERY, GRAD, VALUE)
    ] + [pltpu.make_async_copy(o_ref, saved, load_sem.at[4])]
    for load in loads:
        load.start()

    barrier = pltpu.get_barrier_semaphore()

    def greet(s, j):
        pl.semaphore_signal(
            barrier, inc=1, device_id=(j, shifted(s), group), device_id_type=MESH
        )

    for s in order:
        each_peer(s, greet)
    planes = sum(jnp.where(inside[s], 1, 0) for s in range(n_slot))
    pl.semaphore_wait(barrier, planes * n_ta - 1)

    start_span(KEY, centre)
    start_planes(KEY, 0)
    for a in (KEY, VALUE, QUERY, GRAD):
        start_pair(a, centre, 0)

    for s in others:

        @pl.when(jnp.logical_not(inside[s]))
        def _(s=s):
            for a in (KEY, QUERY, GRAD, VALUE):
                near[a, s] = jnp.zeros(near.shape[2:], bf16)
            stats[s] = jnp.zeros(stats.shape[1:], f32)

    for load in loads:
        load.wait()

    head_of = [slice(h * HEAD_DIM, (h + 1) * HEAD_DIM) for h in range(heads)]
    column = lax.broadcasted_iota(jnp.int32, (1, keys), 1)
    def mine(a, h):
        return near[a, centre, time, :, head_of[h]]

    row_dot = [
        jnp.sum(
            mine(GRAD, h).astype(f32) * saved[:, head_of[h]].astype(f32),
            axis=-1,
            keepdims=True,
        )
        for h in range(heads)
    ]

    def tile_time(j):
        return j * frames_dev // TILE_T

    def open_bias(s, as_query):
        dr, dc = moves[s]
        bias = jnp.full((1, keys), -jnp.inf, f32)
        for j in range(n_ta):
            if as_query:
                query_time, time_step = tile_time(time), tile_time(j) - tile_time(time)
                query_row, query_col, row_step, col_step = row_tile, col_tile, dr, dc
            else:
                query_time, time_step = tile_time(j), tile_time(time) - tile_time(j)
                query_row = jnp.clip(row_tile + dr, 0, row_tiles - 1)
                query_col = jnp.clip(col_tile + dc, 0, col_tiles - 1)
                row_step, col_step = -dr, -dc
            close = (time_step >= -1) & (time_step <= 1)
            code = (jnp.clip(time_step, -1, 1) + 1) * 9 + (row_step + 1) * 3 + (col_step + 1)
            is_open = (mask_ref[query_time, query_row, query_col, code] == 1) & close & inside[s]
            here = (column >= j * rows) & (column < (j + 1) * rows)
            bias = jnp.where(here & is_open, 0.0, bias)
        return bias

    def dot(a, b, dims):
        return lax.dot_general(a, b, (dims, ((), ())), preferred_element_type=f32)

    def block_of(a, s, h):
        return near[a, s, :, :, head_of[h]].reshape(keys, HEAD_DIM)

    slot_max = {}
    slot_sum = {}

    def fold(values, combine):
        parts = [values[:, at : at + 128] for at in range(0, step, 128)]
        return functools.reduce(combine, parts)

    def own_scores(s):
        bias = open_bias(s, True)
        for h in range(heads):
            query, near_keys = mine(QUERY, h), block_of(KEY, s, h)
            tops = []
            for c in chunks:
                scores = dot(query, near_keys[c], ((1,), (1,))) + bias[:, c]
                raised[s, h, :, c] = scores
                tops.append(fold(scores, jnp.maximum))
            top = functools.reduce(jnp.maximum, tops)
            top = jnp.maximum(jnp.max(top, axis=-1, keepdims=True), LOWEST)
            sums = []
            for c in chunks:
                lifted = jnp.exp2((raised[s, h, :, c] - top) * to_two)
                raised[s, h, :, c] = lifted
                sums.append(fold(lifted, jnp.add))
            total = functools.reduce(jnp.add, sums)
            slot_max[s, h] = top
            slot_sum[s, h] = jnp.sum(total, axis=-1, keepdims=True)

    pass_on_span(KEY)
    start_span(VALUE, centre)
    wait_rest(KEY, centre)
    own_scores(centre)
    start_planes(VALUE, 0)
    start_planes(QUERY, 0)
    start_span(QUERY, centre)
    for s in others:
        for d in range(n_high):
            pass_on_planes(KEY, s, d)
    for s in others:
        wait_rest(KEY, s)
        own_scores(s)
        if s == others[0]:
            pass_on_span(VALUE)
            start_span(GRAD, centre)

    factor = {}
    columns = []
    for h in range(heads):
        top = slot_max[centre, h]
        for s in others:
            top = jnp.maximum(top, slot_max[s, h])
        gain = {s: jnp.exp2((slot_max[s, h] - top) * to_two) for s in order}
        total = gain[centre] * slot_sum[centre, h]
        for s in others:
            total = total + gain[s] * slot_sum[s, h]
        for s in order:
            factor[s, h] = gain[s] * (scale / total)
        columns.append(top * to_two + jnp.log2(total))
    columns = columns + row_dot
    lane = lax.broadcasted_iota(jnp.int32, (rows, HEAD_DIM), 1)
    table = jnp.zeros((rows, HEAD_DIM), f32)
    for index, col in enumerate(columns):
        table = jnp.where(lane == index, col, table)
    stats[centre, time] = table.T[: stats.shape[2]]
    for s in order:
        each_peer(s, lambda s, j: stat_copy(s, j).start())

    def stat_rows(s):
        return jnp.concatenate([stats[s, j] for j in range(n_ta)], axis=1)

    def key_weights(s):
        each_peer(s, stat_arrived)
        bias = open_bias(s, False)
        table = stat_rows(s)
        for h in range(heads):
            key, queries = mine(KEY, h), block_of(QUERY, s, h)
            shift = bias - table[h : h + 1]
            for c in chunks:
                scores = dot(key, queries[c], ((1,), (1,)))
                lifted_own[s, h, :, c] = jnp.exp2(scores * to_two + shift[:, c])

    def add(acc, h, first, part):
        if first:
            acc[:, head_of[h]] = part
        else:
            acc[:, head_of[h]] += part

    def key_grads(s):
        table = stat_rows(s)
        for h in range(heads):
            grads, queries, value = block_of(GRAD, s, h), block_of(QUERY, s, h), mine(VALUE, h)
            shift = table[heads + h : heads + h + 1]
            value_part = key_part = 0.0
            for c in chunks:
                weights = lifted_own[s, h, :, c]
                value_part += dot(weights.astype(bf16), grads[c], ((1,), (0,)))
                weight_grad = dot(value, grads[c], ((1,), (1,)))
                score_grad = (weights * (weight_grad - shift[:, c])).astype(bf16)
                key_part += dot(score_grad, queries[c], ((1,), (0,)))
            add(dv_acc, h, s == centre, value_part)
            add(dk_acc, h, s == centre, key_part)

    def query_grads(s):
        for h in range(heads):
            grad, values, near_keys = mine(GRAD, h), block_of(VALUE, s, h), block_of(KEY, s, h)
            query_part = 0.0
            for c in chunks:
                weight_grad = dot(grad, values[c], ((1,), (1,)))
                score_grad = (raised[s, h, :, c] * (weight_grad - row_dot[h])).astype(bf16)
                query_part += dot(score_grad, near_keys[c], ((1,), (0,)))
            add(dq_acc, h, s == centre, query_part * factor[s, h])

    pass_on_span(QUERY)
    for s in others:
        pass_on_planes(QUERY, s, 0)
    start_planes(GRAD, 0)
    wait_rest(VALUE, centre)
    query_grads(centre)
    pass_on_span(GRAD)
    for s in others:
        pass_on_planes(VALUE, s, 0)
    wait_rest(QUERY, centre)
    key_weights(centre)
    wait_rest(GRAD, centre)
    key_grads(centre)
    for s in others:
        for d in range(1, n_high):
            pass_on_planes(VALUE, s, d)
    for s in others:
        wait_rest(VALUE, s)
        query_grads(s)
    dq_ref[...] = dq_acc[...].astype(bf16)
    for s in others:
        pass_on_planes(GRAD, s, 0)
        for d in range(1, n_high):
            pass_on_planes(QUERY, s, d)
    for s in others:
        wait_rest(QUERY, s)
        key_weights(s)
    for s in others:
        for d in range(1, n_high):
            pass_on_planes(GRAD, s, d)
    for s in others:
        wait_rest(GRAD, s)
        key_grads(s)
    dk_ref[...] = (dk_acc[...] * scale).astype(bf16)
    dv_ref[...] = dv_acc[...].astype(bf16)

    for a in (KEY, QUERY, GRAD, VALUE):
        for s in order:

            def finish(s=s, a=a):
                for d in range(n_high):
                    if s != centre and (d == 0 or a not in ACROSS_SPAN):
                        plane_copy(a, s, d).wait_send()
                    if d != 0 and (s == centre or a in ACROSS_SPAN):
                        span_copy(a, s, d).wait_send()
                    if n_low == 2:
                        pair_copy(a, s, d).wait_send()

            if_inside(s, finish)
    for s in order:
        each_peer(s, lambda s, j: stat_copy(s, j).wait_send())


def write_results(dq_ref, dk_ref, dv_ref, query_grad, key_grad, value_grad):
    query_grad[...] = dq_ref[...]
    key_grad[...] = dk_ref[...]
    value_grad[...] = dv_ref[...]


def local(n_ta, query_in, key_in, value_in, saved_out, out_grad, window_mask):
    f32, bf16 = jnp.float32, jnp.bfloat16
    shape = query_in.shape
    frames_dev, _, tile_rows, tile_cols, width = shape
    rows = frames_dev * tile_rows * tile_cols
    heads = width // HEAD_DIM
    _, row_tiles, col_tiles, _ = window_mask.shape
    moves = [
        (dr, dc)
        for dr in (-1, 0, 1)
        for dc in (-1, 0, 1)
        if abs(dr) < row_tiles and abs(dc) < col_tiles
    ]
    n_slot = len(moves)
    dims = (n_ta, row_tiles, col_tiles, frames_dev, heads, moves)
    vmem = pl.BlockSpec(memory_space=pltpu.VMEM)
    out = jax.ShapeDtypeStruct((rows, width), bf16)
    stat_rows = -(-2 * heads // 8) * 8
    weights = pltpu.VMEM((n_slot, heads, rows, n_ta * rows), f32)
    total = pltpu.VMEM((rows, width), f32)
    dma = pltpu.SemaphoreType.DMA
    kept = pl.BlockSpec(memory_space=pl.ANY)
    results = pl.pallas_call(
        functools.partial(kernel, dims),
        out_shape=(out, out, out),
        in_specs=[pl.BlockSpec(memory_space=pltpu.SMEM)] + [kept] * 5,
        out_specs=(vmem, vmem, vmem),
        scratch_shapes=[
            pltpu.VMEM((4, n_slot, n_ta, rows, width), bf16),
            pltpu.VMEM((n_slot, n_ta, stat_rows, rows), f32),
            weights,
            weights,
            total,
            total,
            total,
            pltpu.VMEM((rows, width), bf16),
            dma((5,)),
            dma((4, n_slot, n_ta)),
            dma((4, n_slot, n_ta)),
            dma((4, n_slot, n_ta)),
            dma((4, n_slot, n_ta)),
            dma((n_slot, n_ta)),
            dma((n_slot, n_ta)),
        ],
        compiler_params=pltpu.CompilerParams(
            collective_id=0, has_side_effects=True, vmem_limit_bytes=56 * 1024 * 1024
        ),
    )(
        window_mask,
        *(x.reshape(rows, width) for x in (query_in, key_in, value_in, saved_out, out_grad)),
    )
    results = pl.pallas_call(
        write_results,
        out_shape=(out, out, out),
        in_specs=[vmem] * 3,
        out_specs=(vmem, vmem, vmem),
    )(*results)
    return tuple(x.reshape(shape) for x in results)


def solution(mesh):
    spec = P("ta", "ha", None, None, "ga")
    return jax.shard_map(
        functools.partial(local, mesh.shape["ta"]),
        mesh=mesh,
        in_specs=(spec, spec, spec, spec, spec, P()),
        out_specs=(spec, spec, spec),
        check_vma=False,
    )
```

```python
import functools

import jax
import jax.numpy as jnp
from jax import lax
from jax.experimental import pallas as pl
from jax.experimental.pallas import tpu as pltpu
from jax.sharding import PartitionSpec as P

HEAD_DIM = 128
TILE_T = 6
LOG2_E = 1.4426950408889634
LOWEST = -1e30
MESH = pl.DeviceIdType.MESH
KEY, QUERY, GRAD, VALUE = range(4)
ACROSS_SPAN = (QUERY,)


def kernel(
    dims,
    mask_ref,
    q_ref,
    k_ref,
    v_ref,
    o_ref,
    g_ref,
    dq_ref,
    dk_ref,
    dv_ref,
    near,
    stats,
    raised,
    lifted_own,
    dq_acc,
    dk_acc,
    dv_acc,
    saved,
    load_sem,
    sent,
    pair_sem,
    recv_sem,
    stat_send,
    stat_recv,
):
    f32, bf16 = jnp.float32, jnp.bfloat16
    n_ta, row_tiles, col_tiles, frames_dev, heads, moves = dims
    rows = saved.shape[0]
    n_slot = len(moves)
    centre = moves.index((0, 0))
    others = [s for s in range(n_slot) if s != centre]
    order = [centre] + others
    keys = n_ta * rows
    step = 256 if keys % 256 == 0 else keys
    chunks = [slice(at, at + step) for at in range(0, keys, step)]
    scale = HEAD_DIM ** (-0.5)
    to_two = scale * LOG2_E
    n_low = 2 if n_ta % 2 == 0 else 1
    n_high = n_ta // n_low

    time = lax.axis_index("ta")
    plane = lax.axis_index("ha")
    group = lax.axis_index("ga")
    high, low = time // n_low, time % n_low
    row_tile = plane // col_tiles
    col_tile = plane % col_tiles
    inside = [
        (row_tile + dr >= 0)
        & (row_tile + dr < row_tiles)
        & (col_tile + dc >= 0)
        & (col_tile + dc < col_tiles)
        for dr, dc in moves
    ]
    own = {KEY: k_ref, QUERY: q_ref, GRAD: g_ref, VALUE: v_ref}

    def shifted(s):
        dr, dc = moves[s]
        return plane + dr * col_tiles + dc

    def back(s):
        return n_slot - 1 - s

    def if_inside(s, do):
        if s == centre:
            do()
        else:
            pl.when(inside[s])(do)

    def place_of(t):
        return t % n_low * n_high + t // n_low

    def time_of(p):
        return p % n_high * n_low + p // n_high

    here = place_of(time)
    chain = low * n_high
    across = (1 - low) * n_high

    def push(src, dst, send_sem, recv_sem, device):
        return pltpu.make_async_remote_copy(
            src_ref=src,
            dst_ref=dst,
            send_sem=send_sem,
            recv_sem=recv_sem,
            device_id=device,
            device_id_type=MESH,
        )

    def arrival(block, sem):
        push(block, block, sem, sem, (time, plane, group)).wait_recv()

    def chain_place(d):
        return chain + (high + d) % n_high

    def start_span(a, s):
        src = own[a] if s == centre else near.at[a, s, here]
        for d in range(1, n_high):
            j = (high + d) % n_high * n_low + low
            push(
                src, near.at[a, s, here], sent.at[a, s], recv_sem.at[a, s, here], (j, plane, group)
            ).start()

    def start_planes(a, d):
        p = chain_place(d)
        src = own[a] if d == 0 else near.at[a, centre, p]
        for s in others:

            @pl.when(inside[s])
            def _(s=s):
                device = (time, shifted(s), group)
                r = back(s)
                push(
                    src, near.at[a, r, p], sent.at[a, s], recv_sem.at[a, r, p], device
                ).start()

    def start_pair(a, s, src, dst):
        if n_low == 2:
            device = (high * n_low + 1 - low, plane, group)
            push(src, dst, sent.at[a, s], pair_sem.at[a, s], device).start()

    def chain_arrived(a, s, d):
        p = chain_place(d)
        arrival(near.at[a, s, p], recv_sem.at[a, s, p])

    def pass_on_span(a):
        for d in range(1, n_high):
            chain_arrived(a, centre, d)
            if a not in ACROSS_SPAN:
                start_planes(a, d)
            block = near.at[a, centre, chain_place(d)]
            start_pair(a, centre, block, block)

    def span_planes(a):
        for s in others:

            @pl.when(inside[s])
            def _(s=s):
                chain_arrived(a, s, 0)
                start_span(a, s)

    def pass_on_planes(a):
        for s in others:

            @pl.when(inside[s])
            def _(s=s):
                for d in range(n_high):
                    if d != 0 or a not in ACROSS_SPAN:
                        chain_arrived(a, s, d)
                blocks = near.at[a, s, pl.ds(chain, n_high)]
                start_pair(a, s, blocks, blocks)

    def wait_rest(a, s):
        if n_low == 2:
            if_inside(
                s, lambda: arrival(near.at[a, s, pl.ds(across, n_high)], pair_sem.at[a, s])
            )

    def peers(s):
        if s == centre:
            return [(time + d) % n_ta for d in range(1, n_ta)]
        return list(range(n_ta))

    def send_stats(s):
        def do():
            for j in peers(s):
                push(
                    stats.at[centre, here],
                    stats.at[back(s), here],
                    stat_send.at[s],
                    stat_recv.at[back(s)],
                    (j, shifted(s), group),
                ).start()

        if_inside(s, do)

    def stats_of(s):
        return stats.at[s, pl.ds(0, len(peers(s)))]

    loads = [
        pltpu.make_async_copy(own[a], near.at[a, centre, here], load_sem.at[a])
        for a in (KEY, QUERY, GRAD, VALUE)
    ] + [pltpu.make_async_copy(o_ref, saved, load_sem.at[4])]
    for load in loads:
        load.start()

    barrier = pltpu.get_barrier_semaphore()

    def greet(s):
        for j in peers(s):
            pl.semaphore_signal(
                barrier, inc=1, device_id=(j, shifted(s), group), device_id_type=MESH
            )

    for s in order:
        if_inside(s, functools.partial(greet, s))
    planes = sum(jnp.where(inside[s], 1, 0) for s in range(n_slot))
    pl.semaphore_wait(barrier, planes * n_ta - 1)

    start_span(KEY, centre)
    start_planes(KEY, 0)
    for a in (KEY, VALUE, QUERY, GRAD):
        start_pair(a, centre, own[a], near.at[a, centre, here])

    for s in others:

        @pl.when(jnp.logical_not(inside[s]))
        def _(s=s):
            for a in (KEY, QUERY, GRAD, VALUE):
                near[a, s] = jnp.zeros(near.shape[2:], bf16)
            stats[s] = jnp.zeros(stats.shape[1:], f32)

    for load in loads:
        load.wait()

    head_of = [slice(h * HEAD_DIM, (h + 1) * HEAD_DIM) for h in range(heads)]
    column = lax.broadcasted_iota(jnp.int32, (1, keys), 1)

    def mine(a, h):
        return near[a, centre, here, :, head_of[h]]

    row_dot = [
        jnp.sum(
            mine(GRAD, h).astype(f32) * saved[:, head_of[h]].astype(f32),
            axis=-1,
            keepdims=True,
        )
        for h in range(heads)
    ]

    def tile_time(j):
        return j * frames_dev // TILE_T

    def open_bias(s, as_query):
        dr, dc = moves[s]
        bias = jnp.full((1, keys), -jnp.inf, f32)
        for p in range(n_ta):
            j = time_of(p)
            if as_query:
                query_time, time_step = tile_time(time), tile_time(j) - tile_time(time)
                query_row, query_col, row_step, col_step = row_tile, col_tile, dr, dc
            else:
                query_time, time_step = tile_time(j), tile_time(time) - tile_time(j)
                query_row = jnp.clip(row_tile + dr, 0, row_tiles - 1)
                query_col = jnp.clip(col_tile + dc, 0, col_tiles - 1)
                row_step, col_step = -dr, -dc
            close = (time_step >= -1) & (time_step <= 1)
            code = (jnp.clip(time_step, -1, 1) + 1) * 9 + (row_step + 1) * 3 + (col_step + 1)
            is_open = (mask_ref[query_time, query_row, query_col, code] == 1) & close & inside[s]
            block = (column >= p * rows) & (column < (p + 1) * rows)
            bias = jnp.where(block & is_open, 0.0, bias)
        return bias

    def dot(a, b, dims):
        return lax.dot_general(a, b, (dims, ((), ())), preferred_element_type=f32)

    def block_of(a, s, h):
        return near[a, s, :, :, head_of[h]].reshape(keys, HEAD_DIM)

    slot_max = {}
    slot_sum = {}

    def fold(values, combine):
        parts = [values[:, at : at + 128] for at in range(0, step, 128)]
        return functools.reduce(combine, parts)

    def own_scores(s):
        bias = open_bias(s, True)
        for h in range(heads):
            query, near_keys = mine(QUERY, h), block_of(KEY, s, h)
            tops = []
            for c in chunks:
                scores = dot(query, near_keys[c], ((1,), (1,))) + bias[:, c]
                raised[s, h, :, c] = scores
                tops.append(fold(scores, jnp.maximum))
            top = functools.reduce(jnp.maximum, tops)
            top = jnp.maximum(jnp.max(top, axis=-1, keepdims=True), LOWEST)
            sums = []
            for c in chunks:
                lifted = jnp.exp2((raised[s, h, :, c] - top) * to_two)
                raised[s, h, :, c] = lifted
                sums.append(fold(lifted, jnp.add))
            total = functools.reduce(jnp.add, sums)
            slot_max[s, h] = top
            slot_sum[s, h] = jnp.sum(total, axis=-1, keepdims=True)

    pass_on_span(KEY)
    start_span(VALUE, centre)
    wait_rest(KEY, centre)
    own_scores(centre)
    start_planes(VALUE, 0)
    start_planes(QUERY, 0)
    start_span(QUERY, centre)
    pass_on_planes(KEY)
    for s in others:
        wait_rest(KEY, s)
        own_scores(s)
        if s == others[0]:
            pass_on_span(VALUE)
            start_span(GRAD, centre)

    factor = {}
    columns = []
    for h in range(heads):
        top = slot_max[centre, h]
        for s in others:
            top = jnp.maximum(top, slot_max[s, h])
        gain = {s: jnp.exp2((slot_max[s, h] - top) * to_two) for s in order}
        total = gain[centre] * slot_sum[centre, h]
        for s in others:
            total = total + gain[s] * slot_sum[s, h]
        for s in order:
            factor[s, h] = gain[s] * (scale / total)
        columns.append(top * to_two + jnp.log2(total))
    columns = columns + row_dot
    lane = lax.broadcasted_iota(jnp.int32, (rows, HEAD_DIM), 1)
    table = jnp.zeros((rows, HEAD_DIM), f32)
    for index, col in enumerate(columns):
        table = jnp.where(lane == index, col, table)
    stats[centre, here] = table.T[: stats.shape[2]]
    for s in order:
        send_stats(s)

    def stat_rows(s):
        return jnp.concatenate([stats[s, j] for j in range(n_ta)], axis=1)

    def key_weights(s):
        bias = open_bias(s, False)
        table = stat_rows(s)
        for h in range(heads):
            key, queries = mine(KEY, h), block_of(QUERY, s, h)
            shift = bias - table[h : h + 1]
            for c in chunks:
                scores = dot(key, queries[c], ((1,), (1,)))
                lifted_own[s, h, :, c] = jnp.exp2(scores * to_two + shift[:, c])

    def add(acc, h, first, part):
        if first:
            acc[:, head_of[h]] = part
        else:
            acc[:, head_of[h]] += part

    def key_grads(s):
        table = stat_rows(s)
        for h in range(heads):
            grads, queries, value = block_of(GRAD, s, h), block_of(QUERY, s, h), mine(VALUE, h)
            shift = table[heads + h : heads + h + 1]
            value_part = key_part = 0.0
            for c in chunks:
                weights = lifted_own[s, h, :, c]
                value_part += dot(weights.astype(bf16), grads[c], ((1,), (0,)))
                weight_grad = dot(value, grads[c], ((1,), (1,)))
                score_grad = (weights * (weight_grad - shift[:, c])).astype(bf16)
                key_part += dot(score_grad, queries[c], ((1,), (0,)))
            add(dv_acc, h, s == centre, value_part)
            add(dk_acc, h, s == centre, key_part)

    def query_grads(s):
        for h in range(heads):
            grad, values, near_keys = mine(GRAD, h), block_of(VALUE, s, h), block_of(KEY, s, h)
            query_part = 0.0
            for c in chunks:
                weight_grad = dot(grad, values[c], ((1,), (1,)))
                score_grad = (raised[s, h, :, c] * (weight_grad - row_dot[h])).astype(bf16)
                query_part += dot(score_grad, near_keys[c], ((1,), (0,)))
            add(dq_acc, h, s == centre, query_part * factor[s, h])

    def wait_stats(s):
        if_inside(s, lambda: arrival(stats_of(s), stat_recv.at[s]))

    pass_on_span(QUERY)
    span_planes(QUERY)
    start_planes(GRAD, 0)
    wait_rest(VALUE, centre)
    query_grads(centre)
    pass_on_span(GRAD)
    pass_on_planes(VALUE)
    wait_rest(QUERY, centre)
    wait_rest(GRAD, centre)
    wait_stats(centre)
    key_weights(centre)
    key_grads(centre)
    for s in others:
        wait_rest(VALUE, s)
    for s in others:
        query_grads(s)
    dq_ref[...] = dq_acc[...].astype(bf16)
    pass_on_planes(QUERY)
    for s in others:
        wait_rest(QUERY, s)
        wait_stats(s)
    for s in others:
        key_weights(s)
    pass_on_planes(GRAD)
    for s in others:
        wait_rest(GRAD, s)
    for s in others:
        key_grads(s)
    dk_ref[...] = (dk_acc[...] * scale).astype(bf16)
    dv_ref[...] = dv_acc[...].astype(bf16)

    def all_sent(s):
        count = (n_high if n_low == 1 else n_ta) - (1 if s == centre else 0)
        for a in (KEY, QUERY, GRAD, VALUE):
            block = near.at[a, s, pl.ds(0, count)]
            push(block, block, sent.at[a, s], sent.at[a, s], (time, plane, group)).wait_send()
        block = stats_of(s)
        push(
            block, block, stat_send.at[s], stat_send.at[s], (time, plane, group)
        ).wait_send()

    for s in order:
        if_inside(s, functools.partial(all_sent, s))


def write_results(dq_ref, dk_ref, dv_ref, query_grad, key_grad, value_grad):
    query_grad[...] = dq_ref[...]
    key_grad[...] = dk_ref[...]
    value_grad[...] = dv_ref[...]


def local(n_ta, query_in, key_in, value_in, saved_out, out_grad, window_mask):
    f32, bf16 = jnp.float32, jnp.bfloat16
    shape = query_in.shape
    frames_dev, _, tile_rows, tile_cols, width = shape
    rows = frames_dev * tile_rows * tile_cols
    heads = width // HEAD_DIM
    _, row_tiles, col_tiles, _ = window_mask.shape
    moves = [
        (dr, dc)
        for dr in (-1, 0, 1)
        for dc in (-1, 0, 1)
        if abs(dr) < row_tiles and abs(dc) < col_tiles
    ]
    n_slot = len(moves)
    dims = (n_ta, row_tiles, col_tiles, frames_dev, heads, moves)
    vmem = pl.BlockSpec(memory_space=pltpu.VMEM)
    out = jax.ShapeDtypeStruct((rows, width), bf16)
    stat_rows = -(-2 * heads // 8) * 8
    weights = pltpu.VMEM((n_slot, heads, rows, n_ta * rows), f32)
    total = pltpu.VMEM((rows, width), f32)
    dma = pltpu.SemaphoreType.DMA
    kept = pl.BlockSpec(memory_space=pl.ANY)
    results = pl.pallas_call(
        functools.partial(kernel, dims),
        out_shape=(out, out, out),
        in_specs=[pl.BlockSpec(memory_space=pltpu.SMEM)] + [kept] * 5,
        out_specs=(vmem, vmem, vmem),
        scratch_shapes=[
            pltpu.VMEM((4, n_slot, n_ta, rows, width), bf16),
            pltpu.VMEM((n_slot, n_ta, stat_rows, rows), f32),
            weights,
            weights,
            total,
            total,
            total,
            pltpu.VMEM((rows, width), bf16),
            dma((5,)),
            dma((4, n_slot)),
            dma((4, n_slot)),
            dma((4, n_slot, n_ta)),
            dma((n_slot,)),
            dma((n_slot,)),
        ],
        compiler_params=pltpu.CompilerParams(
            collective_id=0, has_side_effects=True, vmem_limit_bytes=56 * 1024 * 1024
        ),
    )(
        window_mask,
        *(x.reshape(rows, width) for x in (query_in, key_in, value_in, saved_out, out_grad)),
    )
    results = pl.pallas_call(
        write_results,
        out_shape=(out, out, out),
        in_specs=[vmem] * 3,
        out_specs=(vmem, vmem, vmem),
    )(*results)
    return tuple(x.reshape(shape) for x in results)


def solution(mesh):
    spec = P("ta", "ha", None, None, "ga")
    return jax.shard_map(
        functools.partial(local, mesh.shape["ta"]),
        mesh=mesh,
        in_specs=(spec, spec, spec, spec, spec, P()),
        out_specs=(spec, spec, spec),
        check_vma=False,
    )
```

```python
import functools

import jax
import jax.numpy as jnp
from jax import lax
from jax.experimental import pallas as pl
from jax.experimental.pallas import tpu as pltpu
from jax.sharding import PartitionSpec as P

HEAD_DIM = 128
TILE_T = 6
LOG2_E = 1.4426950408889634
LOWEST = -1e30
MESH = pl.DeviceIdType.MESH
KEY, QUERY, GRAD, VALUE = range(4)
ACROSS_SPAN = (QUERY,)


def kernel(
    dims,
    mask_ref,
    q_ref,
    k_ref,
    v_ref,
    o_ref,
    g_ref,
    dq_ref,
    dk_ref,
    dv_ref,
    near,
    stats,
    raised,
    lifted_own,
    dq_acc,
    dk_acc,
    dv_acc,
    saved,
    load_sem,
    sent,
    pair_sem,
    recv_sem,
    stat_send,
    stat_recv,
):
    f32, bf16 = jnp.float32, jnp.bfloat16
    n_ta, row_tiles, col_tiles, frames_dev, heads, moves = dims
    rows = saved.shape[0]
    n_slot = len(moves)
    centre = moves.index((0, 0))
    others = [s for s in range(n_slot) if s != centre]
    order = [centre] + others
    keys = n_ta * rows
    step = 256 if keys % 256 == 0 else keys
    chunks = [slice(at, at + step) for at in range(0, keys, step)]
    scale = HEAD_DIM ** (-0.5)
    to_two = scale * LOG2_E
    n_low = 2 if n_ta % 2 == 0 else 1
    n_high = n_ta // n_low

    time = lax.axis_index("ta")
    plane = lax.axis_index("ha")
    group = lax.axis_index("ga")
    high, low = time // n_low, time % n_low
    row_tile = plane // col_tiles
    col_tile = plane % col_tiles
    inside = [
        (row_tile + dr >= 0)
        & (row_tile + dr < row_tiles)
        & (col_tile + dc >= 0)
        & (col_tile + dc < col_tiles)
        for dr, dc in moves
    ]
    own = {KEY: k_ref, QUERY: q_ref, GRAD: g_ref, VALUE: v_ref}

    def shifted(s):
        dr, dc = moves[s]
        return plane + dr * col_tiles + dc

    def back(s):
        return n_slot - 1 - s

    def if_inside(s, do):
        if s == centre:
            do()
        else:
            pl.when(inside[s])(do)

    def place_of(t):
        return t % n_low * n_high + t // n_low

    def time_of(p):
        return p % n_high * n_low + p // n_high

    here = place_of(time)
    chain = low * n_high
    across = (1 - low) * n_high

    def push(src, dst, send_sem, recv_sem, device):
        return pltpu.make_async_remote_copy(
            src_ref=src,
            dst_ref=dst,
            send_sem=send_sem,
            recv_sem=recv_sem,
            device_id=device,
            device_id_type=MESH,
        )

    def arrival(block, sem):
        push(block, block, sem, sem, (time, plane, group)).wait_recv()

    def chain_place(d):
        return chain + (high + d) % n_high

    def start_span(a, s):
        src = own[a] if s == centre else near.at[a, s, here]
        for d in range(1, n_high):
            j = (high + d) % n_high * n_low + low
            push(
                src, near.at[a, s, here], sent.at[a, s], recv_sem.at[a, s, here], (j, plane, group)
            ).start()

    def start_planes(a, d):
        p = chain_place(d)
        src = own[a] if d == 0 else near.at[a, centre, p]
        for s in others:

            @pl.when(inside[s])
            def _(s=s):
                device = (time, shifted(s), group)
                r = back(s)
                push(
                    src, near.at[a, r, p], sent.at[a, s], recv_sem.at[a, r, p], device
                ).start()

    def start_pair(a, s, src, dst):
        if n_low == 2:
            device = (high * n_low + 1 - low, plane, group)
            push(src, dst, sent.at[a, s], pair_sem.at[a, s], device).start()

    def chain_arrived(a, s, d):
        p = chain_place(d)
        arrival(near.at[a, s, p], recv_sem.at[a, s, p])

    def pass_on_span(a):
        for d in range(1, n_high):
            chain_arrived(a, centre, d)
            if a not in ACROSS_SPAN:
                start_planes(a, d)
            block = near.at[a, centre, chain_place(d)]
            start_pair(a, centre, block, block)

    def span_planes(a):
        for s in others:

            @pl.when(inside[s])
            def _(s=s):
                chain_arrived(a, s, 0)
                start_span(a, s)

    def pass_on_planes(a):
        for s in others:

            @pl.when(inside[s])
            def _(s=s):
                for d in range(n_high):
                    if d != 0 or a not in ACROSS_SPAN:
                        chain_arrived(a, s, d)
                blocks = near.at[a, s, pl.ds(chain, n_high)]
                start_pair(a, s, blocks, blocks)

    def wait_rest(a, s):
        if n_low == 2:
            if_inside(
                s, lambda: arrival(near.at[a, s, pl.ds(across, n_high)], pair_sem.at[a, s])
            )

    def peers(s):
        if s == centre:
            return [(time + d) % n_ta for d in range(1, n_ta)]
        return list(range(n_ta))

    def send_stats(s):
        def do():
            for j in peers(s):
                push(
                    stats.at[centre, here],
                    stats.at[back(s), here],
                    stat_send.at[s],
                    stat_recv.at[back(s)],
                    (j, shifted(s), group),
                ).start()

        if_inside(s, do)

    def stats_of(s):
        return stats.at[s, pl.ds(0, len(peers(s)))]

    loads = [
        pltpu.make_async_copy(own[a], near.at[a, centre, here], load_sem.at[a])
        for a in (KEY, QUERY, GRAD, VALUE)
    ] + [pltpu.make_async_copy(o_ref, saved, load_sem.at[4])]
    for load in loads:
        load.start()

    barrier = pltpu.get_barrier_semaphore()

    def greet(s):
        for j in peers(s):
            pl.semaphore_signal(
                barrier, inc=1, device_id=(j, shifted(s), group), device_id_type=MESH
            )

    for s in order:
        if_inside(s, functools.partial(greet, s))
    planes = sum(jnp.where(inside[s], 1, 0) for s in range(n_slot))
    pl.semaphore_wait(barrier, planes * n_ta - 1)

    start_span(KEY, centre)
    start_planes(KEY, 0)
    for a in (KEY, VALUE, QUERY, GRAD):
        start_pair(a, centre, own[a], near.at[a, centre, here])

    for s in others:

        @pl.when(jnp.logical_not(inside[s]))
        def _(s=s):
            for a in (KEY, QUERY, GRAD, VALUE):
                near[a, s] = jnp.zeros(near.shape[2:], bf16)
            stats[s] = jnp.zeros(stats.shape[1:], f32)

    for load in loads:
        load.wait()

    head_of = [slice(h * HEAD_DIM, (h + 1) * HEAD_DIM) for h in range(heads)]
    column = lax.broadcasted_iota(jnp.int32, (1, keys), 1)

    def mine(a, h):
        return near[a, centre, here, :, head_of[h]]

    row_dot = [
        jnp.sum(
            mine(GRAD, h).astype(f32) * saved[:, head_of[h]].astype(f32),
            axis=-1,
            keepdims=True,
        )
        for h in range(heads)
    ]

    def tile_time(j):
        return j * frames_dev // TILE_T

    def open_bias(s, as_query):
        dr, dc = moves[s]
        bias = jnp.full((1, keys), -jnp.inf, f32)
        for p in range(n_ta):
            j = time_of(p)
            if as_query:
                query_time, time_step = tile_time(time), tile_time(j) - tile_time(time)
                query_row, query_col, row_step, col_step = row_tile, col_tile, dr, dc
            else:
                query_time, time_step = tile_time(j), tile_time(time) - tile_time(j)
                query_row = jnp.clip(row_tile + dr, 0, row_tiles - 1)
                query_col = jnp.clip(col_tile + dc, 0, col_tiles - 1)
                row_step, col_step = -dr, -dc
            close = (time_step >= -1) & (time_step <= 1)
            code = (jnp.clip(time_step, -1, 1) + 1) * 9 + (row_step + 1) * 3 + (col_step + 1)
            is_open = (mask_ref[query_time, query_row, query_col, code] == 1) & close & inside[s]
            block = (column >= p * rows) & (column < (p + 1) * rows)
            bias = jnp.where(block & is_open, 0.0, bias)
        return bias

    def dot(a, b, dims):
        return lax.dot_general(a, b, (dims, ((), ())), preferred_element_type=f32)

    def block_of(a, s, h):
        return near[a, s, :, :, head_of[h]].reshape(keys, HEAD_DIM)

    slot_max = {}
    slot_sum = {}

    def fold(values, combine):
        parts = [values[:, at : at + 128] for at in range(0, step, 128)]
        return functools.reduce(combine, parts)

    def own_scores(s):
        bias = open_bias(s, True)
        for h in range(heads):
            query, near_keys = mine(QUERY, h), block_of(KEY, s, h)
            tops = []
            for c in chunks:
                scores = dot(query, near_keys[c], ((1,), (1,))) + bias[:, c]
                raised[s, h, :, c] = scores
                tops.append(fold(scores, jnp.maximum))
            top = functools.reduce(jnp.maximum, tops)
            top = jnp.maximum(jnp.max(top, axis=-1, keepdims=True), LOWEST)
            sums = []
            for c in chunks:
                lifted = jnp.exp2((raised[s, h, :, c] - top) * to_two)
                raised[s, h, :, c] = lifted
                sums.append(fold(lifted, jnp.add))
            total = functools.reduce(jnp.add, sums)
            slot_max[s, h] = top
            slot_sum[s, h] = jnp.sum(total, axis=-1, keepdims=True)

    pass_on_span(KEY)
    start_span(VALUE, centre)
    wait_rest(KEY, centre)
    own_scores(centre)
    start_planes(VALUE, 0)
    start_planes(QUERY, 0)
    start_span(QUERY, centre)
    pass_on_planes(KEY)
    for s in others:
        wait_rest(KEY, s)
        own_scores(s)
        if s == others[0]:
            pass_on_span(VALUE)
            start_span(GRAD, centre)
            start_planes(GRAD, 0)

    factor = {}
    columns = []
    for h in range(heads):
        top = slot_max[centre, h]
        for s in others:
            top = jnp.maximum(top, slot_max[s, h])
        gain = {s: jnp.exp2((slot_max[s, h] - top) * to_two) for s in order}
        total = gain[centre] * slot_sum[centre, h]
        for s in others:
            total = total + gain[s] * slot_sum[s, h]
        for s in order:
            factor[s, h] = gain[s] * (scale / total)
        columns.append(top * to_two + jnp.log2(total))
    columns = columns + row_dot
    lane = lax.broadcasted_iota(jnp.int32, (rows, HEAD_DIM), 1)
    table = jnp.zeros((rows, HEAD_DIM), f32)
    for index, col in enumerate(columns):
        table = jnp.where(lane == index, col, table)
    stats[centre, here] = table.T[: stats.shape[2]]
    for s in order:
        send_stats(s)

    def stat_rows(s):
        return jnp.concatenate([stats[s, j] for j in range(n_ta)], axis=1)

    def key_weights(s):
        bias = open_bias(s, False)
        table = stat_rows(s)
        for h in range(heads):
            key, queries = mine(KEY, h), block_of(QUERY, s, h)
            shift = bias - table[h : h + 1]
            for c in chunks:
                scores = dot(key, queries[c], ((1,), (1,)))
                lifted_own[s, h, :, c] = jnp.exp2(scores * to_two + shift[:, c])

    def add(acc, h, first, part):
        if first:
            acc[:, head_of[h]] = part
        else:
            acc[:, head_of[h]] += part

    def key_grads(s):
        table = stat_rows(s)
        for h in range(heads):
            grads, queries, value = block_of(GRAD, s, h), block_of(QUERY, s, h), mine(VALUE, h)
            shift = table[heads + h : heads + h + 1]
            value_part = key_part = 0.0
            for c in chunks:
                weights = lifted_own[s, h, :, c]
                value_part += dot(weights.astype(bf16), grads[c], ((1,), (0,)))
                weight_grad = dot(value, grads[c], ((1,), (1,)))
                score_grad = (weights * (weight_grad - shift[:, c])).astype(bf16)
                key_part += dot(score_grad, queries[c], ((1,), (0,)))
            add(dv_acc, h, s == centre, value_part)
            add(dk_acc, h, s == centre, key_part)

    def query_grads(s):
        for h in range(heads):
            grad, values, near_keys = mine(GRAD, h), block_of(VALUE, s, h), block_of(KEY, s, h)
            query_part = 0.0
            for c in chunks:
                weight_grad = dot(grad, values[c], ((1,), (1,)))
                score_grad = (raised[s, h, :, c] * (weight_grad - row_dot[h])).astype(bf16)
                query_part += dot(score_grad, near_keys[c], ((1,), (0,)))
            add(dq_acc, h, s == centre, query_part * factor[s, h])

    def wait_stats(s):
        if_inside(s, lambda: arrival(stats_of(s), stat_recv.at[s]))

    pass_on_span(QUERY)
    span_planes(QUERY)
    pass_on_span(GRAD)
    wait_rest(VALUE, centre)
    query_grads(centre)
    pass_on_planes(VALUE)
    wait_rest(QUERY, centre)
    wait_rest(GRAD, centre)
    wait_stats(centre)
    key_weights(centre)
    key_grads(centre)
    for s in others:
        wait_rest(VALUE, s)
        query_grads(s)
        if s == others[0]:
            pass_on_planes(QUERY)
    dq_ref[...] = dq_acc[...].astype(bf16)
    pass_on_planes(GRAD)
    for s in others:
        wait_rest(QUERY, s)
        wait_stats(s)
    for s in others:
        key_weights(s)
    for s in others:
        wait_rest(GRAD, s)
    for s in others:
        key_grads(s)
    dk_ref[...] = (dk_acc[...] * scale).astype(bf16)
    dv_ref[...] = dv_acc[...].astype(bf16)

    def all_sent(s):
        count = (n_high if n_low == 1 else n_ta) - (1 if s == centre else 0)
        for a in (KEY, QUERY, GRAD, VALUE):
            block = near.at[a, s, pl.ds(0, count)]
            push(block, block, sent.at[a, s], sent.at[a, s], (time, plane, group)).wait_send()
        block = stats_of(s)
        push(
            block, block, stat_send.at[s], stat_send.at[s], (time, plane, group)
        ).wait_send()

    for s in order:
        if_inside(s, functools.partial(all_sent, s))


def write_results(dq_ref, dk_ref, dv_ref, query_grad, key_grad, value_grad):
    query_grad[...] = dq_ref[...]
    key_grad[...] = dk_ref[...]
    value_grad[...] = dv_ref[...]


def local(n_ta, query_in, key_in, value_in, saved_out, out_grad, window_mask):
    f32, bf16 = jnp.float32, jnp.bfloat16
    shape = query_in.shape
    frames_dev, _, tile_rows, tile_cols, width = shape
    rows = frames_dev * tile_rows * tile_cols
    heads = width // HEAD_DIM
    _, row_tiles, col_tiles, _ = window_mask.shape
    moves = [
        (dr, dc)
        for dr in (-1, 0, 1)
        for dc in (-1, 0, 1)
        if abs(dr) < row_tiles and abs(dc) < col_tiles
    ]
    n_slot = len(moves)
    dims = (n_ta, row_tiles, col_tiles, frames_dev, heads, moves)
    vmem = pl.BlockSpec(memory_space=pltpu.VMEM)
    out = jax.ShapeDtypeStruct((rows, width), bf16)
    stat_rows = -(-2 * heads // 8) * 8
    weights = pltpu.VMEM((n_slot, heads, rows, n_ta * rows), f32)
    total = pltpu.VMEM((rows, width), f32)
    dma = pltpu.SemaphoreType.DMA
    kept = pl.BlockSpec(memory_space=pl.ANY)
    results = pl.pallas_call(
        functools.partial(kernel, dims),
        out_shape=(out, out, out),
        in_specs=[pl.BlockSpec(memory_space=pltpu.SMEM)] + [kept] * 5,
        out_specs=(vmem, vmem, vmem),
        scratch_shapes=[
            pltpu.VMEM((4, n_slot, n_ta, rows, width), bf16),
            pltpu.VMEM((n_slot, n_ta, stat_rows, rows), f32),
            weights,
            weights,
            total,
            total,
            total,
            pltpu.VMEM((rows, width), bf16),
            dma((5,)),
            dma((4, n_slot)),
            dma((4, n_slot)),
            dma((4, n_slot, n_ta)),
            dma((n_slot,)),
            dma((n_slot,)),
        ],
        compiler_params=pltpu.CompilerParams(
            collective_id=0, has_side_effects=True, vmem_limit_bytes=56 * 1024 * 1024
        ),
    )(
        window_mask,
        *(x.reshape(rows, width) for x in (query_in, key_in, value_in, saved_out, out_grad)),
    )
    results = pl.pallas_call(
        write_results,
        out_shape=(out, out, out),
        in_specs=[vmem] * 3,
        out_specs=(vmem, vmem, vmem),
    )(*results)
    return tuple(x.reshape(shape) for x in results)


def solution(mesh):
    spec = P("ta", "ha", None, None, "ga")
    return jax.shard_map(
        functools.partial(local, mesh.shape["ta"]),
        mesh=mesh,
        in_specs=(spec, spec, spec, spec, spec, P()),
        out_specs=(spec, spec, spec),
        check_vma=False,
    )
```
